256 devices in a mesh: loop: 32 (over y, z_lo, core), rows: 8 (over z_hi, x).
Axes of the slice: x: 4, y: 4, z: 8 (z_hi: 2, z_lo: 4; z = z_hi * 4 + z_lo), core: 2. Of those that a mesh axis runs over, the one named last changes fastest.
Arguments:
- load: bfloat16 [262144, 128], P(('loop', 'rows')), may hold values from -6 to 6
- cluster_perm: int32 [2048, 128], P(('loop', 'rows')), may hold values from 0 to 127, each once within a row
- near_blocks: bfloat16 [98304, 128, 128], P(('loop', 'rows')), may hold values from -0.078125 to 0.078125
- near_index: int32 [98304, 2], P(('loop', 'rows')), may hold values from 0 to 2047, as said below
- near_live: int32 [256], P(('loop', 'rows')), may hold values from 96 to 384, as said below
- col_basis: bfloat16 [2048, 16, 128], P(('loop', 'rows')), may hold values from -0.5 to 0.5
- row_basis: bfloat16 [2048, 16, 128], P(('loop', 'rows')), may hold values from -1.5 to 1.5
- far_couple: bfloat16 [16384, 16, 16], P(('loop', 'rows')), may hold values from -0.5 to 0.5
- far_index: int32 [16384, 2], P(('loop', 'rows')), may hold values from 0 to 2047, as said below
Outputs:
- response: bfloat16 [262144, 128], P(('loop', 'rows'))
The draws below stay inside these ranges and needn't reach their ends.
Inputs may be any that keep to these rules, and one draw needn't show every extreme that they name: `near_index`: slot b belongs to device b // 384, whose loop index is (b // 384) // 8. Column 0 is the block's row tile among that device's 8 tiles; column 1 is a column tile whose loop index (tile // 64) differs from the holder's loop index by at most 2. `near_live`: the number of leading live slots of each device; later slots are ignored. Some device has all 384 live in every draw. `far_index`: pair p belongs to device p // 64. Column 0 is the row tile among that device's 8 tiles; column 1 is a column tile held by any device. `cluster_perm`: each row is a permutation.
All inputs are finite; a program needn't handle non-finite values.
Results may differ from the reference program's by a relative error of at most 0.014.
Values may be sent and summed in bfloat16 or wider, within the bound.
A program may use at most 128 MiB of HBM per device.

```python
import jax
import jax.numpy as jnp
from jax import lax

BS = 128
NRHS = 128
RK = 16
REACH = 2
TPD = 8
NB = 384
NF = 64
LOOP_LEN = 32
ROW_LEN = 8
NDEV = 256
TPL = 64
NT = 2048
M = 262144
NB_ALL = 98304
NF_ALL = 16384


def draw_near_index(key, part):
    keys = jax.random.split(jax.random.fold_in(key, 11), 3)
    loop_pos = jnp.arange(NB_ALL, dtype=jnp.int32) // NB // ROW_LEN
    lower = jnp.maximum(loop_pos - REACH, 0)
    upper = jnp.minimum(loop_pos + REACH, LOOP_LEN - 1)
    row_tile = jax.random.randint(keys[0], (NB_ALL,), 0, TPD, dtype=jnp.int32)
    col_loop = jax.random.randint(keys[1], (NB_ALL,), lower, upper + 1, dtype=jnp.int32)
    col_tile = col_loop * TPL + jax.random.randint(keys[2], (NB_ALL,), 0, TPL, dtype=jnp.int32)
    return jnp.stack([row_tile, col_tile], axis=-1).astype(jnp.int32)


def draw_near_live(key, part):
    keys = jax.random.split(jax.random.fold_in(key, 23), 2)
    counts = jax.random.randint(keys[0], (NDEV,), NB // 4, NB + 1, dtype=jnp.int32)
    chosen = jax.random.randint(keys[1], (), 0, NDEV, dtype=jnp.int32)
    return jnp.where(jnp.arange(NDEV, dtype=jnp.int32) == chosen, NB, counts).astype(jnp.int32)


def draw_far_index(key, part):
    keys = jax.random.split(jax.random.fold_in(key, 37), 4)
    holder = jnp.arange(NF_ALL, dtype=jnp.int32) // NF
    slot = jnp.arange(NF_ALL, dtype=jnp.int32) % NF
    loop_pos = holder // ROW_LEN
    row_tile = jax.random.randint(keys[0], (NF_ALL,), 0, TPD, dtype=jnp.int32)
    offset = jax.random.randint(keys[1], (NF_ALL,), REACH + 1, LOOP_LEN - REACH, dtype=jnp.int32)
    col_loop = (loop_pos + offset) % LOOP_LEN
    far_tile = col_loop * TPL + jax.random.randint(keys[2], (NF_ALL,), 0, TPL, dtype=jnp.int32)
    before = (holder + NDEV - 1) % NDEV * TPD + jax.random.randint(keys[3], (NF_ALL,), 0, TPD, dtype=jnp.int32)
    col_tile = jnp.where(slot == 0, before, far_tile)
    return jnp.stack([row_tile, col_tile], axis=-1).astype(jnp.int32)


def levels(own_key, dims, cuts, low, high):
    loudness, own = 1.0, jax.random.fold_in(own_key, 6)
    for axis_at, parts in cuts:
        steps = jnp.exp(jax.random.uniform(jax.random.fold_in(own, axis_at), (parts,), jnp.float32, low / len(cuts), high / len(cuts)))
        loudness = loudness * jnp.repeat(steps, dims[axis_at] // parts).reshape([-1 if axis == axis_at else 1 for axis in range(len(dims))])
    return loudness


def scatter_about(stream_key, shape, spread, limit, cuts=(), kind=jnp.bfloat16):
    loudness = levels(stream_key, shape, cuts, -0.22, 0.18) if cuts else 1.0
    result = jax.random.normal(stream_key, shape, jnp.float32) * spread * loudness
    return jnp.minimum(jnp.maximum(result, -limit), limit).astype(kind)


def setup_inputs(seed: int = 0) -> dict:
    splits = jax.random.split(jax.random.key(seed), 10)
    load = scatter_about(splits[0], (M, NRHS), 1.0, 6.0, ((0, 256),))
    cluster_perm = jax.vmap(lambda own: jax.random.permutation(own, BS))(jax.random.split(splits[1], NT)).reshape((NT, BS)).astype(jnp.int32)
    near_blocks = scatter_about(splits[2], (NB_ALL, BS, BS), (BS * NB // TPD) ** -0.5, 0.078125, ((0, 256),))
    near_index = draw_near_index(jax.random.fold_in(splits[9], 71), 0)
    near_live = draw_near_live(jax.random.fold_in(splits[9], 71), 0)
    col_basis = scatter_about(splits[5], (NT, RK, BS), BS ** -0.5, 0.5, ((0, 256),))
    row_basis = scatter_about(splits[6], (NT, RK, BS), RK ** -0.5, 1.5, ((0, 256),))
    far_couple = scatter_about(splits[7], (NF_ALL, RK, RK), (RK * NF // TPD) ** -0.5, 0.5, ((0, 256),))
    far_index = draw_far_index(jax.random.fold_in(splits[9], 71), 0)
    return dict(load=load, cluster_perm=cluster_perm, near_blocks=near_blocks, near_index=near_index, near_live=near_live, col_basis=col_basis, row_basis=row_basis, far_couple=far_couple, far_index=far_index)


def reference(load, cluster_perm, near_blocks, near_index, near_live, col_basis, row_basis, far_couple, far_index):
    grid = load.reshape(NT, BS, NRHS)
    clustered = jax.vmap(lambda tile_rows, order: tile_rows[order])(grid, cluster_perm)

    def device_near(device):
        start = (device * NB).astype(jnp.int32)
        blocks = lax.dynamic_slice_in_dim(near_blocks, start, NB, 0).astype(jnp.float32)
        index = lax.dynamic_slice_in_dim(near_index, start, NB, 0)
        chosen = jnp.take(clustered, index[:, 1], axis=0).astype(jnp.float32)
        product = jnp.einsum("gij,gjn->gin", blocks, chosen)
        live = jnp.arange(NB, dtype=jnp.int32) < near_live[device]
        product = jnp.where(live[:, None, None], product, jnp.zeros_like(product))
        return jax.ops.segment_sum(product, index[:, 0], num_segments=TPD)

    near_sum = lax.map(device_near, jnp.arange(NDEV, dtype=jnp.int32)).reshape(NT, BS, NRHS)
    coeffs = jnp.einsum("trb,tbn->trn", col_basis.astype(jnp.float32), clustered.astype(jnp.float32)).astype(jnp.bfloat16)
    picked = jnp.take(coeffs, far_index[:, 1], axis=0).astype(jnp.float32)
    contrib = jnp.einsum("prk,pkn->prn", far_couple.astype(jnp.float32), picked)
    target = (jnp.arange(NF_ALL, dtype=jnp.int32) // NF) * TPD + far_index[:, 0]
    far_coeffs = jax.ops.segment_sum(contrib, target, num_segments=NT).astype(jnp.bfloat16)
    far_part = jnp.einsum("trb,trn->tbn", row_basis.astype(jnp.float32), far_coeffs.astype(jnp.float32))
    total = (near_sum + far_part).astype(jnp.bfloat16)
    placed = jax.vmap(lambda values, order: jnp.zeros_like(values).at[order].set(values))(total, cluster_perm)
    return placed.reshape(M, NRHS)
```

```python
import functools

import jax
import jax.numpy as jnp
from jax import lax
from jax.experimental import pallas as pl
from jax.experimental.pallas import tpu as pltpu
from jax.sharding import PartitionSpec as P

MESH = pl.DeviceIdType.MESH
VMEM = pltpu.VMEM
TILES, LEN, CASES, RANK = 8, 128, 128, 16
BLOCKS, PAIRS = 384, 64
CHUNK = 32


def turn_matrix(order):
    rows = lax.broadcasted_iota(jnp.int32, (LEN, LEN), 0)
    return jnp.where(rows == order, 1.0, 0.0).astype(jnp.bfloat16)


def prep_kernel(load, perm, basis, clustered, coeffs):
    for t in range(TILES):
        turn = turn_matrix(perm[t : t + 1, :])
        tile = lax.dot_general(
            turn, load[t], (((0,), (0,)), ((), ())), preferred_element_type=jnp.float32
        ).astype(jnp.bfloat16)
        clustered[t] = tile
        coeffs[t] = jnp.dot(basis[t], tile, preferred_element_type=jnp.float32).astype(jnp.bfloat16)


def share_kernel(own, coef, band, far, send, recv, local_sem):
    loop, rows = lax.axis_index("loop"), lax.axis_index("rows")
    core, column = loop % 2, loop // 2
    zlo, y = column % 4, column // 4
    zhi, x = rows // 4, rows % 4
    other = 1 - zhi
    xn, xb = (x + 1) % 4, (x + 3) % 4
    zn, zb = (zlo + 1) % 4, (zlo + 3) % 4
    yn, yb = (y + 1) % 4, (y + 3) % 4
    x2, z2, y2 = (x + 2) % 4, (zlo + 2) % 4, (y + 2) % 4
    over = (zhi + (zlo + 1) // 4) % 2
    under = (zhi + 1 - (zlo + 3) // 4) % 2

    def device(at, side, high, across):
        return (at * 2 + side, high * 4 + across)

    opposite = device(column, core, other, x)
    x_up = device(column, core, zhi, xn)
    x_down = device(column, core, zhi, xb)
    z_up = device(y * 4 + zn, core, over, x)
    z_down = device(y * 4 + zb, core, under, x)
    h_up = device((column + 1) % 16, core, over, x)
    h_down = device((column + 15) % 16, core, under, x)
    y_up = device(yn * 4 + zlo, core, zhi, x)
    y_down = device(yb * 4 + zlo, core, zhi, x)
    sibling = device(column, 1 - core, zhi, x)

    barrier = pltpu.get_barrier_semaphore()
    peers = (opposite, x_up, x_down, z_up, z_down, h_up, h_down, y_up, y_down, sibling)
    for peer in peers:
        pl.semaphore_signal(barrier, inc=1, device_id=peer, device_id_type=MESH)
    pl.semaphore_wait(barrier, len(peers))

    started = []
    pending = set()

    def put(src, dst, to):
        k = len(started)
        copy = pltpu.make_async_remote_copy(
            src_ref=src,
            dst_ref=dst,
            send_sem=send.at[k],
            recv_sem=recv.at[k],
            device_id=to,
            device_id_type=MESH,
        )
        copy.start()
        started.append(copy)
        pending.add(k)
        return k

    def got(*ks):
        for k in ks:
            if k in pending:
                started[k].wait_recv()
                pending.discard(k)

    def relay(ref, to):
        return put(ref, ref, to)

    own_far = far.at[y, zlo, core, zhi, x]
    fo = put(coef, own_far, opposite)
    fxu = put(coef, own_far, x_up)
    fxd = put(coef, own_far, x_down)
    keep_far = pltpu.make_async_copy(coef, own_far, local_sem.at[0])
    keep_far.start()
    own_near = band.at[1, core, zhi, x]
    no = put(own, own_near, opposite)
    nxu = put(own, own_near, x_up)
    nxd = put(own, own_near, x_down)
    nhu = put(own, band.at[0, core, zhi, x], h_up)
    nhd = put(own, band.at[2, core, zhi, x], h_down)
    keep_near = pltpu.make_async_copy(own, own_near, local_sem.at[1])
    keep_near.start()

    got(fo)
    opp_far = far.at[y, zlo, core, other, x]
    fxu2 = relay(opp_far, x_up)
    fxd2 = relay(opp_far, x_down)
    got(fxu, fxu2)
    ffu = relay(far.at[y, zlo, core, 0, xb], x_up)
    got(fxd, fxd2)
    ffd = relay(far.at[y, zlo, core, 1, xn], x_down)

    got(no)
    opp_near = band.at[1, core, other, x]
    nxu2 = relay(opp_near, x_up)
    nxd2 = relay(opp_near, x_down)
    nhu2 = put(opp_near, band.at[0, core, other, x], h_up)
    nhd2 = put(opp_near, band.at[2, core, other, x], h_down)

    got(ffu, ffd)
    keep_far.wait()
    cols = {}

    def spread(at):
        cols[at] = (relay(far.at[y, at_of[at], core], y_up), relay(far.at[y, at_of[at], core], y_down))
        relay(far.at[y, at_of[at], core], sibling)

    at_of = {"own": zlo, "before": zb, "after": zn, "two": z2}
    fzu = relay(far.at[y, zlo, core], z_up)
    fzd = relay(far.at[y, zlo, core], z_down)
    spread("own")

    got(nxd, nxd2)
    nfd = relay(band.at[1, core, 1, xn], x_down)
    nhu3 = put(band.at[1, core, :, xn], band.at[0, core, :, xn], h_up)
    nhd3 = put(band.at[1, core, :, xn], band.at[2, core, :, xn], h_down)
    got(nxu, nxu2)
    nfu = relay(band.at[1, core, 0, xb], x_up)

    got(fzu)
    ffzu = relay(far.at[y, zb, core, 0], z_up)
    got(fzd)
    ffzd = relay(far.at[y, zn, core, 1], z_down)
    spread("before")
    spread("after")

    got(nhu, nhu2)
    nau = relay(band.at[0, core, :, x], x_up)
    got(nhd, nhd2)
    nbu = relay(band.at[2, core, :, x], x_up)

    got(ffzu, ffzd)
    spread("two")

    side = 2 - 2 * core
    keep_near.wait()
    relay(band.at[1, core, :, x], sibling)
    relay(band.at[1, core, :, xn], sibling)
    relay(band.at[1, core, :, xb], sibling)
    relay(band.at[side, core, :, x], sibling)

    forward = []

    def onward(at):
        up, down = cols[at]
        got(up)
        forward.append(relay(far.at[yb, at_of[at], core, 0], y_up))
        relay(far.at[yb, at_of[at], core], sibling)
        got(down)
        forward.append(relay(far.at[yn, at_of[at], core, 1], y_down))
        relay(far.at[yn, at_of[at], core], sibling)

    onward("own")
    got(nhu3)
    nad = relay(band.at[0, core, :, xn], x_down)
    got(nhd3)
    nbd = relay(band.at[2, core, :, xn], x_down)
    relay(band.at[side, core, :, xn], sibling)
    onward("before")
    onward("after")
    got(nfu, nfd)
    relay(band.at[1, core, :, x2], sibling)
    onward("two")
    got(nau, nbu)
    relay(band.at[side, core, :, xb], sibling)
    got(nad, nbd)
    relay(band.at[side, core, :, x2], sibling)
    for n, at in enumerate(("own", "before", "after", "two")):
        got(forward[2 * n], forward[2 * n + 1])
        relay(far.at[y2, at_of[at], core], sibling)

    for k in range(len(started)):
        got(k)
    for copy in started:
        copy.wait_send()


def apply_kernel(
    near_index, near_live, far_index,
    blocks, band, coeffs, couple, basis, perm,
    out,
    band_v, blocks_v, picked, total, band_sem, block_sem, pick_sem,
):
    loop = lax.axis_index("loop")
    core = loop % 2
    live = near_live[0]
    first = (loop - 2) * 64

    reads = []
    for n in range(5):
        reads.append(
            pltpu.make_async_copy(band.at[core + n], band_v.at[pl.ds(n * 64, 64)], band_sem.at[n])
        )
        reads[-1].start()
    chunks = []
    for n in range(BLOCKS // CHUNK):
        span = pl.ds(n * CHUNK, CHUNK)
        chunks.append(pltpu.make_async_copy(blocks.at[span], blocks_v.at[span], block_sem.at[n]))
        chunks[-1].start()

    @pl.loop(0, PAIRS)
    def _(p):
        tile = jnp.clip(far_index[1, p], 0, 2047)
        pltpu.make_async_copy(coeffs.at[tile], picked.at[p], pick_sem).start()

    total[...] = jnp.zeros_like(total)
    for read in reads:
        read.wait()
    for n in range(BLOCKS // CHUNK):
        chunks[n].wait()

        @pl.when(n * CHUNK < live)
        def _():
            @pl.loop(n * CHUNK // 8, (n + 1) * CHUNK // 8)
            def _(group):
                for k in range(8):
                    b = group * 8 + k
                    row = jnp.where(b < live, jnp.clip(near_index[0, b], 0, TILES - 1), TILES)
                    tile = jnp.clip(near_index[1, b] - first, 0, 319)
                    total[row] += jnp.dot(
                        blocks_v[b], band_v[tile], preferred_element_type=jnp.float32
                    )

    pltpu.make_async_copy(coeffs.at[pl.ds(0, PAIRS)], picked, pick_sem).wait()
    gathered = picked[...].reshape(PAIRS * RANK, CASES)
    far = jnp.dot(couple[...], gathered, preferred_element_type=jnp.float32).astype(jnp.bfloat16)
    for t in range(TILES):
        part = lax.dot_general(
            basis[t], far[t * RANK : (t + 1) * RANK], (((0,), (0,)), ((), ())),
            preferred_element_type=jnp.float32,
        )
        tile = (total[t] + part).astype(jnp.bfloat16)
        placed = jnp.dot(turn_matrix(perm[t : t + 1, :]), tile, preferred_element_type=jnp.float32)
        out[t * LEN : (t + 1) * LEN, :] = placed.astype(jnp.bfloat16)


def local(
    load, cluster_perm, near_blocks, near_index, near_live, col_basis, row_basis, far_couple, far_index
):
    bf16 = jnp.bfloat16
    clustered, coeffs = pl.pallas_call(
        prep_kernel,
        out_shape=(
            jax.ShapeDtypeStruct((TILES, LEN, CASES), bf16),
            jax.ShapeDtypeStruct((TILES, RANK, CASES), bf16),
        ),
        name="prep",
    )(load.reshape(TILES, LEN, CASES), cluster_perm, col_basis)

    anywhere = pl.BlockSpec(memory_space=pl.ANY)
    band, far = pl.pallas_call(
        share_kernel,
        out_shape=(
            jax.ShapeDtypeStruct((3, 2, 2, 4, TILES, LEN, CASES), bf16),
            jax.ShapeDtypeStruct((4, 4, 2, 2, 4, TILES, RANK, CASES), bf16),
        ),
        in_specs=[anywhere, anywhere],
        out_specs=(anywhere, anywhere),
        scratch_shapes=[
            pltpu.SemaphoreType.DMA((96,)),
            pltpu.SemaphoreType.DMA((96,)),
            pltpu.SemaphoreType.DMA((2,)),
        ],
        compiler_params=pltpu.CompilerParams(collective_id=0, has_side_effects=True),
        name="share",
    )(clustered, coeffs)

    owner = far_index[:, 0]
    couple = jnp.transpose(far_couple, (1, 0, 2))
    mask = owner[None, None, :, None] == jnp.arange(TILES, dtype=jnp.int32)[:, None, None, None]
    couple = jnp.where(mask, couple[None], jnp.zeros((), bf16)).reshape(TILES * RANK, PAIRS * RANK)

    smem = pl.BlockSpec(memory_space=pltpu.SMEM)
    vmem = pl.BlockSpec(memory_space=VMEM)
    return pl.pallas_call(
        apply_kernel,
        out_shape=jax.ShapeDtypeStruct((TILES * LEN, CASES), bf16),
        in_specs=[smem, smem, smem, anywhere, anywhere, anywhere, vmem, vmem, vmem],
        out_specs=vmem,
        scratch_shapes=[
            VMEM((320, LEN, CASES), bf16),
            VMEM((BLOCKS, LEN, LEN), bf16),
            VMEM((PAIRS, RANK, CASES), bf16),
            VMEM((TILES + 1, LEN, CASES), jnp.float32),
            pltpu.SemaphoreType.DMA((5,)),
            pltpu.SemaphoreType.DMA((BLOCKS // CHUNK,)),
            pltpu.SemaphoreType.DMA,
        ],
        compiler_params=pltpu.CompilerParams(vmem_limit_bytes=57 * 1024 * 1024),
        name="apply",
    )(
        near_index.T, near_live, far_index.T,
        near_blocks, band.reshape(6, 64, LEN, CASES), far.reshape(2048, RANK, CASES),
        couple, row_basis, cluster_perm,
    )


def solution(mesh):
    both = ("loop", "rows")
    return jax.shard_map(
        local,
        mesh=mesh,
        in_specs=(
            P(both, None), P(both, None), P(both, None, None), P(both, None), P(both),
            P(both, None, None), P(both, None, None), P(both, None, None), P(both, None),
        ),
        out_specs=P(both, None),
        check_vma=False,
    )
```
